32 devices in a mesh: group: 2 (over y), ctx: 8 (over z, x), chan: 2 (over core).
Axes of the slice: x: 2, y: 2, z: 4, core: 2. Of those that a mesh axis runs over, the one named last changes fastest.
Arguments:
- values: bfloat16 [2048, 4096], P(('group', 'ctx'), 'chan'), parts along dimension 0, may hold values from -6 to 6
- pre_gate: bfloat16 [2048, 4096], P(('group', 'ctx'), 'chan'), parts along dimension 0, may hold values from -6 to 6
- post_gate: bfloat16 [2048, 4096], P(('group', 'ctx'), 'chan'), parts along dimension 0, may hold values from -6 to 6
- filter_spectrum: float32 [2, 16, 128, 4096], P(None, 'ctx', None, 'chan'), may hold values from -9 to 9
- skip_gain: float32 [4096], P('chan'), may hold values from 0.5 to 2
- out_weight: bfloat16 [4096, 4096], P('ctx', 'chan'), may hold values from -0.09375 to 0.09375
Outputs:
- projected: bfloat16 [2048, 4096], P(('group', 'ctx'), 'chan'), parts along dimension 0
The draws below stay inside these ranges and needn't reach their ends.
There are 2 independent parts, one for each index of `group`. The reference program is written for one: setup_inputs(seed, part) draws one part's arguments, and reference() takes and returns one part's arrays. A program takes and returns all parts, laid end to end along the dimension named above; an argument that names none is the same for every part. Nothing has to cross between parts.
All inputs are finite; a program needn't handle non-finite values.
Results may differ from the reference program's by a relative error of at most 0.0049.
Values may be sent and summed in bfloat16 or wider, within the bound.
A program may use at most 128 MiB of HBM per device.

```python
import math
import jax
import jax.numpy as jnp
from jax import lax

DM = 4096
CH = 4096
T_DEV = 128
LENGTH = 1024
FREQ_ROWS = 16


def steps_of(own_key, shape, shards, low, largest):
    def one(position, parts):
        steps = jax.random.uniform(jax.random.fold_in(jax.random.fold_in(own_key, 6), position), (parts,), jnp.float32, low / len(shards), largest / len(shards))
        return jnp.repeat(jnp.exp(steps), shape[position] // parts).reshape((-1,) + (1,) * (len(shape) - position - 1))

    loudness = one(*shards[0])
    for cut in shards[1:]:
        loudness = loudness * one(*cut)
    return loudness


def centred(own_key, extent, deviation, reach, cuts=(), kind=jnp.bfloat16):
    result = deviation * jax.random.normal(own_key, extent, jnp.float32)
    if cuts:
        result = result * steps_of(own_key, extent, cuts, -0.22, 0.18)
    return jnp.clip(result, -reach, reach).astype(kind)


def setup_inputs(seed: int = 0, part: int = 0) -> dict:
    key_of = jax.random.split(jax.random.key(seed), 7)
    part_keys = jax.random.split(jax.random.fold_in(key_of[6], part), 7)
    values = centred(part_keys[0], (LENGTH, CH), 1.0, 6.0, ((0, 8), (1, 2)))
    pre_gate = centred(part_keys[1], (LENGTH, CH), 1.0, 6.0, ((0, 8), (1, 2)))
    post_gate = centred(part_keys[2], (LENGTH, CH), 1.0, 6.0, ((0, 8), (1, 2)))
    filter_spectrum = centred(key_of[3], (2, FREQ_ROWS, T_DEV, CH), 1.5, 9.0, ((1, 8), (3, 2)), jnp.float32)
    skip_gain = jnp.clip(jnp.exp(math.log(2.0) - 1.3862944 * jax.random.uniform(key_of[4], (CH,), jnp.float32) ** steps_of(key_of[4], (CH,), ((0, 2),), -0.2, 0.2)), 0.5, 2.0)
    out_weight = centred(key_of[5], (DM, CH), CH ** -0.5, 0.09375, ((0, 8), (1, 2)))
    return dict(values=values, pre_gate=pre_gate, post_gate=post_gate, filter_spectrum=filter_spectrum, skip_gain=skip_gain, out_weight=out_weight)


def reference(values, pre_gate, post_gate, filter_spectrum, skip_gain, out_weight):
    gated_input = values.astype(jnp.float32) * pre_gate.astype(jnp.float32)
    padded_length = 2 * LENGTH
    spectrum_full = jnp.transpose(filter_spectrum, (0, 2, 1, 3)).reshape(2, padded_length, CH)
    block_width = math.gcd(CH, 256)
    block_count = CH // block_width
    gated_blocks = jnp.transpose(gated_input.reshape(LENGTH, block_count, block_width), (1, 0, 2))
    real_blocks = jnp.transpose(spectrum_full[0].reshape(padded_length, block_count, block_width), (1, 0, 2))
    imag_blocks = jnp.transpose(spectrum_full[1].reshape(padded_length, block_count, block_width), (1, 0, 2))

    def convolve_block(inputs):
        gated_block, filter_real, filter_imag = inputs
        forward = jnp.fft.fft(gated_block, n=padded_length, axis=0)
        product = forward * lax.complex(filter_real, filter_imag)
        return jnp.real(jnp.fft.ifft(product, axis=0))[:LENGTH].astype(gated_block.dtype)

    convolved_blocks = lax.map(convolve_block, (gated_blocks, real_blocks, imag_blocks))
    convolved = jnp.transpose(convolved_blocks, (1, 0, 2)).reshape(LENGTH, CH)
    mixer = (post_gate.astype(jnp.float32) * (convolved + skip_gain[None, :] * gated_input)).astype(jnp.bfloat16)
    return jnp.dot(mixer, out_weight.T, preferred_element_type=jnp.float32).astype(jnp.bfloat16)
```

```python
import math

import jax
import jax.numpy as jnp
import numpy as np
from jax import lax
from jax.sharding import PartitionSpec as P

HIGH = lax.Precision.HIGHEST


def trig_table(left_count, right_count, modulus):
    left_ids = jnp.arange(left_count, dtype=jnp.int32)[:, None]
    right_ids = jnp.arange(right_count, dtype=jnp.int32)[None, :]
    angles = (left_ids * right_ids % modulus).astype(jnp.float32) * (2.0 * math.pi / modulus)
    return (jnp.cos(angles), jnp.sin(angles))


def rotate(real_part, imag_part, cosine, sine):
    return (real_part * cosine - imag_part * sine, real_part * sine + imag_part * cosine)


def apply_matrix(matrix, operand):
    return jnp.einsum("kt,...tc->...kc", matrix, operand, precision=HIGH)


def local_transform(real_part, imag_part, direction_sign):
    length_now = real_part.shape[-2]
    cosine, sine = trig_table(length_now, length_now, length_now)
    new_real = apply_matrix(cosine, real_part) - direction_sign * apply_matrix(sine, imag_part)
    new_imag = apply_matrix(cosine, imag_part) + direction_sign * apply_matrix(sine, real_part)
    return (new_real, new_imag)


def twiddle(real_part, imag_part, row_ids, freq_ids, full_length, direction_sign):
    angles = (
        (row_ids * freq_ids % full_length).astype(jnp.float32)
        * (2.0 * math.pi / full_length)
        * direction_sign
    )
    return rotate(real_part, imag_part, jnp.cos(angles), jnp.sin(angles))


def contract_rows(activations, weight_piece):
    return lax.dot_general(
        activations, weight_piece, (((1,), (1,)), ((), ())), preferred_element_type=jnp.float32
    )


def local(values, pre_gate, post_gate, filter_spectrum, skip_gain, out_weight):
    seq_rows, chan_width = values.shape
    ctx_size = lax.axis_size("ctx")
    ctx_index = lax.axis_index("ctx")
    slice_rows = seq_rows // ctx_size
    full_length = 2 * seq_rows * ctx_size
    gated_input = values.astype(jnp.float32) * pre_gate.astype(jnp.float32)
    blocks = lax.all_to_all(
        gated_input.reshape(1, seq_rows, chan_width), "ctx", split_axis=1, concat_axis=0, tiled=True
    )
    flat_blocks = blocks.reshape(ctx_size, slice_rows * chan_width)
    block_cos, block_sin = trig_table(2 * ctx_size, ctx_size, 2 * ctx_size)
    real_part = jnp.dot(block_cos, flat_blocks, precision=HIGH).reshape(
        2 * ctx_size, slice_rows, chan_width
    )
    imag_part = -jnp.dot(block_sin, flat_blocks, precision=HIGH).reshape(
        2 * ctx_size, slice_rows, chan_width
    )
    row_ids = (ctx_index * slice_rows + jnp.arange(slice_rows, dtype=jnp.int32)).reshape(
        1, slice_rows, 1
    )
    freq_ids = jnp.arange(2 * ctx_size, dtype=jnp.int32).reshape(2 * ctx_size, 1, 1)
    real_part, imag_part = twiddle(real_part, imag_part, row_ids, freq_ids, full_length, -1.0)
    columns = lax.all_to_all(
        jnp.stack([real_part, imag_part]), "ctx", split_axis=1, concat_axis=2, tiled=True
    )
    real_part, imag_part = local_transform(columns[0], columns[1], -1.0)
    filter_real = filter_spectrum[0]
    filter_imag = filter_spectrum[1]
    product_real = real_part * filter_real - imag_part * filter_imag
    product_imag = real_part * filter_imag + imag_part * filter_real
    product_real, product_imag = local_transform(product_real, product_imag, 1.0)
    own_freq = (2 * ctx_index + jnp.arange(2, dtype=jnp.int32)).reshape(2, 1, 1)
    all_rows = jnp.arange(seq_rows, dtype=jnp.int32).reshape(1, seq_rows, 1)
    product_real, product_imag = twiddle(
        product_real, product_imag, all_rows, own_freq, full_length, 1.0
    )
    returned_spec = lax.all_to_all(
        jnp.stack([product_real, product_imag]), "ctx", split_axis=2, concat_axis=1, tiled=True
    )
    back_cos, back_sin = trig_table(ctx_size, 2 * ctx_size, 2 * ctx_size)
    spec_real = returned_spec[0].reshape(2 * ctx_size, slice_rows * chan_width)
    spec_imag = returned_spec[1].reshape(2 * ctx_size, slice_rows * chan_width)
    block_out = jnp.dot(back_cos, spec_real, precision=HIGH) - jnp.dot(
        back_sin, spec_imag, precision=HIGH
    )
    block_out = block_out.reshape(ctx_size, slice_rows, chan_width)
    returned = lax.all_to_all(block_out, "ctx", split_axis=0, concat_axis=1, tiled=True)
    convolved = returned.reshape(seq_rows, chan_width) / full_length
    mixer = (post_gate.astype(jnp.float32) * (convolved + skip_gain[None, :] * gated_input)).astype(
        jnp.bfloat16
    )
    partial_value = contract_rows(mixer, lax.all_gather(out_weight, "ctx", axis=0, tiled=True))
    projected = lax.psum_scatter(partial_value, "chan", scatter_dimension=1, tiled=True).astype(
        jnp.bfloat16
    )
    return projected


def dft_tables(residues, quotients, positions):
    full_length = residues * quotients
    kept = residues // 2 + 1
    freq = (np.arange(kept)[:, None] + residues * np.arange(quotients)[None, :]).reshape(-1, 1)
    steps = (freq * np.arange(positions)[None, :]) % full_length
    angles = steps * (2.0 * math.pi / full_length)
    table = np.concatenate([np.cos(angles), -np.sin(angles)], axis=0).astype(np.float32)
    high = table.astype(jnp.bfloat16)
    low = (table - high.astype(np.float32)).astype(jnp.bfloat16)
    return np.concatenate([high, low], axis=1)


def spread(values, pre_gate, post_gate, filter_spectrum, skip_gain, out_weight):
    f32, bf16 = jnp.float32, jnp.bfloat16
    rows, width = values.shape
    groups = lax.axis_size("group")
    ctx_size = lax.axis_size("ctx")
    residues, quotients = 2 * ctx_size, filter_spectrum.shape[2]
    length = rows * ctx_size
    full_length = 2 * length
    mine = width // (groups * ctx_size)
    group_index = lax.axis_index("group")
    ctx_index = lax.axis_index("ctx")
    half = width // groups
    part = lax.dynamic_slice_in_dim(filter_spectrum, group_index * half, half, axis=3)
    part = (part * (1.0 / full_length)).astype(bf16)
    part = part.reshape(2, 2, quotients, ctx_size, mine).transpose(3, 0, 1, 2, 4)
    part = lax.all_to_all(part, "ctx", split_axis=0, concat_axis=0, tiled=True)
    gated = (values.astype(f32) * pre_gate.astype(f32)).astype(bf16)
    pair = jnp.stack([gated, post_gate]).reshape(2, rows, groups * ctx_size, mine).transpose(2, 0, 1, 3)
    pair = lax.all_to_all(pair, ("group", "ctx"), split_axis=0, concat_axis=0, tiled=True)
    pair = pair.reshape(groups, ctx_size, 2, rows, mine).transpose(2, 1, 3, 0, 4)
    pair = pair.reshape(2, length, groups * mine)
    gated, gate = pair[0], pair[1]
    skip = lax.dynamic_slice_in_dim(
        skip_gain, group_index * half + ctx_index * mine, mine, axis=0
    )
    spec = part.transpose(1, 0, 2, 3, 4).reshape(2, residues, quotients, mine)
    middle = residues // 2
    flip = jnp.asarray(np.eye(quotients, dtype=np.float32)[::-1], bf16)
    mirrored = jnp.einsum(
        "qp,xrpc->xrqc", flip, spec[:, :middle:-1], preferred_element_type=f32
    )
    sign = jnp.asarray([1.0, -1.0], f32).reshape(2, 1, 1, 1)
    spec = spec[:, : middle + 1].astype(f32)
    spec = spec + sign * jnp.pad(mirrored, ((0, 0), (1, 1), (0, 0), (0, 0)))
    spec = spec.reshape(2, (middle + 1) * quotients, 1, mine)
    table = jnp.asarray(dft_tables(residues, quotients, length))
    trans = jnp.dot(table, jnp.concatenate([gated, gated], axis=0), preferred_element_type=f32)
    trans = trans.reshape(2, (middle + 1) * quotients, groups, mine)
    product = jnp.stack(
        [trans[0] * spec[0] - trans[1] * spec[1], trans[0] * spec[1] + trans[1] * spec[0]]
    ).astype(bf16)
    product = product.reshape(2 * (middle + 1) * quotients, groups * mine)
    both = lax.dot_general(table, product, (((0,), (0,)), ((), ())), preferred_element_type=f32)
    convolved = both[:length] + both[length:]
    skip = jnp.tile(skip, groups)
    mixer = (gate.astype(f32) * (convolved + skip[None, :] * gated.astype(f32))).astype(bf16)
    mixer = mixer.reshape(length, groups, mine).transpose(1, 0, 2)
    mixer = lax.all_to_all(mixer, "group", split_axis=0, concat_axis=0, tiled=True)
    mixer = lax.all_gather(mixer, "ctx", axis=0)
    mixer = mixer.transpose(2, 1, 0, 3).reshape(length, width)
    partial_value = contract_rows(mixer, out_weight)
    summed = lax.psum_scatter(partial_value, "chan", scatter_dimension=1, tiled=True).astype(bf16)
    chans = lax.axis_size("chan")
    feats = summed.shape[1]
    summed = summed.reshape(ctx_size, rows, feats)
    summed = lax.all_to_all(summed, "ctx", split_axis=0, concat_axis=0, tiled=True)
    summed = summed.reshape(chans, ctx_size // chans, rows, feats)
    summed = lax.all_to_all(summed, "chan", split_axis=0, concat_axis=0, tiled=True)
    return summed.transpose(2, 1, 0, 3).reshape(rows, ctx_size // chans * chans * feats)


def solution(mesh):
    small = mesh.shape["ctx"] <= 8
    return jax.shard_map(
        spread if small else local,
        mesh=mesh,
        in_specs=(
            P(("group", "ctx"), "chan"),
            P(("group", "ctx"), "chan"),
            P(("group", "ctx"), "chan"),
            P(None, "ctx", None, "chan"),
            P("chan"),
            P("ctx", "chan"),
        ),
        out_specs=P(("group", "ctx"), "chan"),
        check_vma=False,
    )
```

```python
import functools
import math

import jax
import jax.numpy as jnp
import numpy as np
from jax import lax
from jax.experimental import pallas as pl
from jax.experimental.pallas import tpu as pltpu
from jax.sharding import PartitionSpec as P

HIGH = lax.Precision.HIGHEST
MESH = pl.DeviceIdType.MESH


def trig_table(left_count, right_count, modulus):
    left_ids = jnp.arange(left_count, dtype=jnp.int32)[:, None]
    right_ids = jnp.arange(right_count, dtype=jnp.int32)[None, :]
    angles = (left_ids * right_ids % modulus).astype(jnp.float32) * (2.0 * math.pi / modulus)
    return (jnp.cos(angles), jnp.sin(angles))


def rotate(real_part, imag_part, cosine, sine):
    return (real_part * cosine - imag_part * sine, real_part * sine + imag_part * cosine)


def apply_matrix(matrix, operand):
    return jnp.einsum("kt,...tc->...kc", matrix, operand, precision=HIGH)


def local_transform(real_part, imag_part, direction_sign):
    length_now = real_part.shape[-2]
    cosine, sine = trig_table(length_now, length_now, length_now)
    new_real = apply_matrix(cosine, real_part) - direction_sign * apply_matrix(sine, imag_part)
    new_imag = apply_matrix(cosine, imag_part) + direction_sign * apply_matrix(sine, real_part)
    return (new_real, new_imag)


def twiddle(real_part, imag_part, row_ids, freq_ids, full_length, direction_sign):
    angles = (
        (row_ids * freq_ids % full_length).astype(jnp.float32)
        * (2.0 * math.pi / full_length)
        * direction_sign
    )
    return rotate(real_part, imag_part, jnp.cos(angles), jnp.sin(angles))


def contract_rows(activations, weight_piece):
    return lax.dot_general(
        activations, weight_piece, (((1,), (1,)), ((), ())), preferred_element_type=jnp.float32
    )


def local(values, pre_gate, post_gate, filter_spectrum, skip_gain, out_weight):
    seq_rows, chan_width = values.shape
    ctx_size = lax.axis_size("ctx")
    ctx_index = lax.axis_index("ctx")
    slice_rows = seq_rows // ctx_size
    full_length = 2 * seq_rows * ctx_size
    gated_input = values.astype(jnp.float32) * pre_gate.astype(jnp.float32)
    blocks = lax.all_to_all(
        gated_input.reshape(1, seq_rows, chan_width), "ctx", split_axis=1, concat_axis=0, tiled=True
    )
    flat_blocks = blocks.reshape(ctx_size, slice_rows * chan_width)
    block_cos, block_sin = trig_table(2 * ctx_size, ctx_size, 2 * ctx_size)
    real_part = jnp.dot(block_cos, flat_blocks, precision=HIGH).reshape(
        2 * ctx_size, slice_rows, chan_width
    )
    imag_part = -jnp.dot(block_sin, flat_blocks, precision=HIGH).reshape(
        2 * ctx_size, slice_rows, chan_width
    )
    row_ids = (ctx_index * slice_rows + jnp.arange(slice_rows, dtype=jnp.int32)).reshape(
        1, slice_rows, 1
    )
    freq_ids = jnp.arange(2 * ctx_size, dtype=jnp.int32).reshape(2 * ctx_size, 1, 1)
    real_part, imag_part = twiddle(real_part, imag_part, row_ids, freq_ids, full_length, -1.0)
    columns = lax.all_to_all(
        jnp.stack([real_part, imag_part]), "ctx", split_axis=1, concat_axis=2, tiled=True
    )
    real_part, imag_part = local_transform(columns[0], columns[1], -1.0)
    filter_real = filter_spectrum[0]
    filter_imag = filter_spectrum[1]
    product_real = real_part * filter_real - imag_part * filter_imag
    product_imag = real_part * filter_imag + imag_part * filter_real
    product_real, product_imag = local_transform(product_real, product_imag, 1.0)
    own_freq = (2 * ctx_index + jnp.arange(2, dtype=jnp.int32)).reshape(2, 1, 1)
    all_rows = jnp.arange(seq_rows, dtype=jnp.int32).reshape(1, seq_rows, 1)
    product_real, product_imag = twiddle(
        product_real, product_imag, all_rows, own_freq, full_length, 1.0
    )
    returned_spec = lax.all_to_all(
        jnp.stack([product_real, product_imag]), "ctx", split_axis=2, concat_axis=1, tiled=True
    )
    back_cos, back_sin = trig_table(ctx_size, 2 * ctx_size, 2 * ctx_size)
    spec_real = returned_spec[0].reshape(2 * ctx_size, slice_rows * chan_width)
    spec_imag = returned_spec[1].reshape(2 * ctx_size, slice_rows * chan_width)
    block_out = jnp.dot(back_cos, spec_real, precision=HIGH) - jnp.dot(
        back_sin, spec_imag, precision=HIGH
    )
    block_out = block_out.reshape(ctx_size, slice_rows, chan_width)
    returned = lax.all_to_all(block_out, "ctx", split_axis=0, concat_axis=1, tiled=True)
    convolved = returned.reshape(seq_rows, chan_width) / full_length
    mixer = (post_gate.astype(jnp.float32) * (convolved + skip_gain[None, :] * gated_input)).astype(
        jnp.bfloat16
    )
    partial_value = contract_rows(mixer, lax.all_gather(out_weight, "ctx", axis=0, tiled=True))
    projected = lax.psum_scatter(partial_value, "chan", scatter_dimension=1, tiled=True).astype(
        jnp.bfloat16
    )
    return projected


PARTS = 4


def project_kernel(
    mixer_ref, weight_ref, out_ref, held, total, share, near, sent, landed,
    y_send, y_recv, z_send, z_recv, own_send, own_recv, pass_send, pass_recv,
    core_send, core_recv, end_send, end_recv, *, lines
):
    ctx_size, groups, length, mine = held.shape
    group = lax.axis_index("group")
    ctx = lax.axis_index("ctx")
    core = lax.axis_index("chan")
    z, x = ctx // 2, ctx % 2
    step = length // PARTS
    rows = length // ctx_size
    feats = weight_ref.shape[0]
    per_core = ctx_size // 2

    def device(ctx_id, core_id):
        return (group, ctx_id, core_id)

    across = (1 - group, ctx, core)
    beside = device(z * 2 + 1 - x, core)
    sibling = device(ctx, 1 - core)

    barrier = pltpu.get_barrier_semaphore()
    pl.semaphore_signal(barrier, inc=1, device_id=across, device_id_type=MESH)
    pl.semaphore_signal(barrier, inc=1, device_id=sibling, device_id_type=MESH)
    for offset in range(1, ctx_size):
        for core_id in range(2):
            pl.semaphore_signal(
                barrier, inc=1, device_id=device(lax.rem(ctx + offset, ctx_size), core_id),
                device_id_type=MESH,
            )
    pl.semaphore_wait(barrier, 2 * ctx_size)

    def remote(src, dst, send, recv, target):
        return pltpu.make_async_remote_copy(
            src_ref=src, dst_ref=dst, send_sem=send, recv_sem=recv, device_id=target,
            device_id_type=MESH,
        )

    def span(part):
        return pl.ds(part * step, step)

    def y_copy(part):
        return remote(
            mixer_ref.at[1 - group, span(part)], held.at[ctx, group, span(part)],
            y_send.at[part], y_recv.at[part], across,
        )

    def z_copy(offset, part):
        return remote(
            held.at[ctx, :, span(part)], held.at[ctx, :, span(part)],
            z_send.at[offset - 1, part], z_recv.at[offset - 1, part],
            device(lax.rem(z + offset, lines) * 2 + x, core),
        )

    def own_copy(part):
        return remote(
            held.at[ctx, :, span(part)], held.at[ctx, :, span(part)],
            own_send.at[part], own_recv.at[part], beside,
        )

    def pass_copy(offset, part):
        source = lax.rem(z + lines - offset, lines) * 2 + x
        return remote(
            held.at[source, :, span(part)], held.at[source, :, span(part)],
            pass_send.at[offset - 1, part], pass_recv.at[offset - 1, part], beside,
        )

    def core_copy(part):
        return remote(
            share.at[part], near.at[part], core_send.at[part], core_recv.at[part], sibling
        )

    slot = lax.rem(ctx, per_core)
    owner = ctx // per_core

    def end_copy(part):
        return remote(
            sent.at[part], landed.at[slot], end_send.at[part], end_recv.at[slot],
            device(2 * part + core, owner),
        )

    for part in range(PARTS):
        y_copy(part).start()
    for part in range(PARTS):
        held[ctx, group, part * step : (part + 1) * step, :] = mixer_ref[
            group, part * step : (part + 1) * step, :
        ]
    for part in range(PARTS):
        y_copy(part).wait_recv()
        for offset in (2, 1, 3):
            z_copy(offset, part).start()
        own_copy(part).start()

    def relay(part):
        for offset in (1, 3, 2):
            z_copy(offset, part).wait_recv()
            pass_copy(offset, part).start()

    def multiply(part):
        own_copy(part).wait_recv()
        for offset in (1, 3, 2):
            pass_copy(offset, part).wait_recv()
        for source in range(ctx_size):
            block = jnp.concatenate(
                [held[source, g, part * step : (part + 1) * step, :] for g in range(groups)], axis=1
            )
            columns = jnp.concatenate(
                [
                    weight_ref[:, (g * ctx_size + source) * mine : (g * ctx_size + source + 1) * mine]
                    for g in range(groups)
                ],
                axis=1,
            )
            term = contract_rows(block, columns)
            if source == 0:
                total[part] = term
            else:
                total[part] += term
        share[part] = total[part, pl.ds(pl.multiple_of((1 - core) * rows, rows), rows), :]
        core_copy(part).start()

    def finish(part):
        core_copy(part).wait_recv()
        mine_part = total[part, pl.ds(pl.multiple_of(core * rows, rows), rows), :]
        sent[part] = (mine_part + near[part]).astype(sent.dtype)
        here = jnp.logical_and(ctx == 2 * part + core, core == owner)

        @pl.when(here)
        def _():
            landed[slot] = sent[part]

        @pl.when(jnp.logical_not(here))
        def _():
            end_copy(part).start()

    relay(0)
    relay(1)
    multiply(0)
    relay(2)
    multiply(1)
    finish(0)
    relay(3)
    multiply(2)
    finish(1)
    multiply(3)
    finish(2)
    finish(3)

    for source in range(per_core):
        from_here = jnp.logical_and(core * per_core + source == ctx, core == lax.rem(ctx, 2))

        @pl.when(jnp.logical_not(from_here))
        def _():
            remote(
                sent.at[0], landed.at[source], end_send.at[0], end_recv.at[source],
                device(0, 0),
            ).wait_recv()

        out_ref[:, source * feats : (source + 1) * feats] = landed[source]

    for part in range(PARTS):
        y_copy(part).wait_send()
        own_copy(part).wait_send()
        core_copy(part).wait_send()
        for offset in range(1, lines):
            z_copy(offset, part).wait_send()
            pass_copy(offset, part).wait_send()
        here = jnp.logical_and(ctx == 2 * part + core, core == owner)

        @pl.when(jnp.logical_not(here))
        def _():
            end_copy(part).wait_send()


def project(mixer, weight, ctx_size):
    groups, length, mine = mixer.shape
    feats = weight.shape[0]
    rows = length // ctx_size
    lines = ctx_size // 2
    dma = pltpu.SemaphoreType.DMA
    return pl.pallas_call(
        functools.partial(project_kernel, lines=lines),
        out_shape=jax.ShapeDtypeStruct((rows, feats * ctx_size // 2), jnp.bfloat16),
        in_specs=[pl.BlockSpec(memory_space=pltpu.VMEM)] * 2,
        out_specs=pl.BlockSpec(memory_space=pltpu.VMEM),
        scratch_shapes=[
            pltpu.VMEM((ctx_size, groups, length, mine), jnp.bfloat16),
            pltpu.VMEM((PARTS, length // PARTS, feats), jnp.float32),
            pltpu.VMEM((PARTS, rows, feats), jnp.float32),
            pltpu.VMEM((PARTS, rows, feats), jnp.float32),
            pltpu.VMEM((PARTS, rows, feats), jnp.bfloat16),
            pltpu.VMEM((ctx_size // 2, rows, feats), jnp.bfloat16),
            dma((PARTS,)), dma((PARTS,)),
            dma((lines - 1, PARTS)), dma((lines - 1, PARTS)),
            dma((PARTS,)), dma((PARTS,)),
            dma((lines - 1, PARTS)), dma((lines - 1, PARTS)),
            dma((PARTS,)), dma((PARTS,)),
            dma((PARTS,)), dma((ctx_size // 2,)),
        ],
        compiler_params=pltpu.CompilerParams(
            collective_id=0, has_side_effects=True, vmem_limit_bytes=40 * 1024 * 1024
        ),
        name="project",
    )(mixer, weight)


def dft_tables(residues, quotients, positions):
    full_length = residues * quotients
    kept = residues // 2 + 1
    freq = (np.arange(kept)[:, None] + residues * np.arange(quotients)[None, :]).reshape(-1, 1)
    steps = (freq * np.arange(positions)[None, :]) % full_length
    angles = steps * (2.0 * math.pi / full_length)
    table = np.concatenate([np.cos(angles), -np.sin(angles)], axis=0).astype(np.float32)
    high = table.astype(jnp.bfloat16)
    low = (table - high.astype(np.float32)).astype(jnp.bfloat16)
    return np.concatenate([high, low], axis=1)


def spread(values, pre_gate, post_gate, filter_spectrum, skip_gain, out_weight):
    f32, bf16 = jnp.float32, jnp.bfloat16
    rows, width = values.shape
    groups = lax.axis_size("group")
    ctx_size = lax.axis_size("ctx")
    residues, quotients = 2 * ctx_size, filter_spectrum.shape[2]
    length = rows * ctx_size
    full_length = 2 * length
    mine = width // (groups * ctx_size)
    group_index = lax.axis_index("group")
    ctx_index = lax.axis_index("ctx")
    half = width // groups
    part = lax.dynamic_slice_in_dim(filter_spectrum, group_index * half, half, axis=3)
    part = (part * (1.0 / full_length)).astype(bf16)
    part = part.reshape(2, 2, quotients, ctx_size, mine).transpose(3, 0, 1, 2, 4)
    part = lax.all_to_all(part, "ctx", split_axis=0, concat_axis=0, tiled=True)
    gated = (values.astype(f32) * pre_gate.astype(f32)).astype(bf16)
    pair = jnp.stack([gated, post_gate]).reshape(2, rows, groups * ctx_size, mine).transpose(2, 0, 1, 3)
    pair = lax.all_to_all(pair, ("group", "ctx"), split_axis=0, concat_axis=0, tiled=True)
    pair = pair.reshape(groups, ctx_size, 2, rows, mine).transpose(2, 1, 3, 0, 4)
    pair = pair.reshape(2, length, groups * mine)
    gated, gate = pair[0], pair[1]
    skip = lax.dynamic_slice_in_dim(
        skip_gain, group_index * half + ctx_index * mine, mine, axis=0
    )
    spec = part.transpose(1, 0, 2, 3, 4).reshape(2, residues, quotients, mine)
    middle = residues // 2
    flip = jnp.asarray(np.eye(quotients, dtype=np.float32)[::-1], bf16)
    mirrored = jnp.einsum(
        "qp,xrpc->xrqc", flip, spec[:, :middle:-1], preferred_element_type=f32
    )
    sign = jnp.asarray([1.0, -1.0], f32).reshape(2, 1, 1, 1)
    spec = spec[:, : middle + 1].astype(f32)
    spec = spec + sign * jnp.pad(mirrored, ((0, 0), (1, 1), (0, 0), (0, 0)))
    spec = spec.reshape(2, (middle + 1) * quotients, 1, mine)
    table = jnp.asarray(dft_tables(residues, quotients, length))
    trans = jnp.dot(table, jnp.concatenate([gated, gated], axis=0), preferred_element_type=f32)
    trans = trans.reshape(2, (middle + 1) * quotients, groups, mine)
    product = jnp.stack(
        [trans[0] * spec[0] - trans[1] * spec[1], trans[0] * spec[1] + trans[1] * spec[0]]
    ).astype(bf16)
    product = product.reshape(2 * (middle + 1) * quotients, groups * mine)
    both = lax.dot_general(table, product, (((0,), (0,)), ((), ())), preferred_element_type=f32)
    convolved = both[:length] + both[length:]
    skip = jnp.tile(skip, groups)
    mixer = (gate.astype(f32) * (convolved + skip[None, :] * gated.astype(f32))).astype(bf16)
    mixer = mixer.reshape(length, groups, mine).transpose(1, 0, 2)
    return project(mixer, out_weight, ctx_size)


def solution(mesh):
    small = mesh.shape["ctx"] <= 8
    return jax.shard_map(
        spread if small else local,
        mesh=mesh,
        in_specs=(
            P(("group", "ctx"), "chan"),
            P(("group", "ctx"), "chan"),
            P(("group", "ctx"), "chan"),
            P(None, "ctx", None, "chan"),
            P("chan"),
            P("ctx", "chan"),
        ),
        out_specs=P(("group", "ctx"), "chan"),
        check_vma=False,
    )
```

```python
import functools
import math

import jax
import jax.numpy as jnp
import numpy as np
from jax import lax
from jax.experimental import pallas as pl
from jax.experimental.pallas import tpu as pltpu
from jax.sharding import PartitionSpec as P

HIGH = lax.Precision.HIGHEST
MESH = pl.DeviceIdType.MESH


def trig_table(left_count, right_count, modulus):
    left_ids = jnp.arange(left_count, dtype=jnp.int32)[:, None]
    right_ids = jnp.arange(right_count, dtype=jnp.int32)[None, :]
    angles = (left_ids * right_ids % modulus).astype(jnp.float32) * (2.0 * math.pi / modulus)
    return (jnp.cos(angles), jnp.sin(angles))


def rotate(real_part, imag_part, cosine, sine):
    return (real_part * cosine - imag_part * sine, real_part * sine + imag_part * cosine)


def apply_matrix(matrix, operand):
    return jnp.einsum("kt,...tc->...kc", matrix, operand, precision=HIGH)


def local_transform(real_part, imag_part, direction_sign):
    length_now = real_part.shape[-2]
    cosine, sine = trig_table(length_now, length_now, length_now)
    new_real = apply_matrix(cosine, real_part) - direction_sign * apply_matrix(sine, imag_part)
    new_imag = apply_matrix(cosine, imag_part) + direction_sign * apply_matrix(sine, real_part)
    return (new_real, new_imag)


def twiddle(real_part, imag_part, row_ids, freq_ids, full_length, direction_sign):
    angles = (
        (row_ids * freq_ids % full_length).astype(jnp.float32)
        * (2.0 * math.pi / full_length)
        * direction_sign
    )
    return rotate(real_part, imag_part, jnp.cos(angles), jnp.sin(angles))


def contract_rows(activations, weight_piece):
    return lax.dot_general(
        activations, weight_piece, (((1,), (1,)), ((), ())), preferred_element_type=jnp.float32
    )


def local(values, pre_gate, post_gate, filter_spectrum, skip_gain, out_weight):
    seq_rows, chan_width = values.shape
    ctx_size = lax.axis_size("ctx")
    ctx_index = lax.axis_index("ctx")
    slice_rows = seq_rows // ctx_size
    full_length = 2 * seq_rows * ctx_size
    gated_input = values.astype(jnp.float32) * pre_gate.astype(jnp.float32)
    blocks = lax.all_to_all(
        gated_input.reshape(1, seq_rows, chan_width), "ctx", split_axis=1, concat_axis=0, tiled=True
    )
    flat_blocks = blocks.reshape(ctx_size, slice_rows * chan_width)
    block_cos, block_sin = trig_table(2 * ctx_size, ctx_size, 2 * ctx_size)
    real_part = jnp.dot(block_cos, flat_blocks, precision=HIGH).reshape(
        2 * ctx_size, slice_rows, chan_width
    )
    imag_part = -jnp.dot(block_sin, flat_blocks, precision=HIGH).reshape(
        2 * ctx_size, slice_rows, chan_width
    )
    row_ids = (ctx_index * slice_rows + jnp.arange(slice_rows, dtype=jnp.int32)).reshape(
        1, slice_rows, 1
    )
    freq_ids = jnp.arange(2 * ctx_size, dtype=jnp.int32).reshape(2 * ctx_size, 1, 1)
    real_part, imag_part = twiddle(real_part, imag_part, row_ids, freq_ids, full_length, -1.0)
    columns = lax.all_to_all(
        jnp.stack([real_part, imag_part]), "ctx", split_axis=1, concat_axis=2, tiled=True
    )
    real_part, imag_part = local_transform(columns[0], columns[1], -1.0)
    filter_real = filter_spectrum[0]
    filter_imag = filter_spectrum[1]
    product_real = real_part * filter_real - imag_part * filter_imag
    product_imag = real_part * filter_imag + imag_part * filter_real
    product_real, product_imag = local_transform(product_real, product_imag, 1.0)
    own_freq = (2 * ctx_index + jnp.arange(2, dtype=jnp.int32)).reshape(2, 1, 1)
    all_rows = jnp.arange(seq_rows, dtype=jnp.int32).reshape(1, seq_rows, 1)
    product_real, product_imag = twiddle(
        product_real, product_imag, all_rows, own_freq, full_length, 1.0
    )
    returned_spec = lax.all_to_all(
        jnp.stack([product_real, product_imag]), "ctx", split_axis=2, concat_axis=1, tiled=True
    )
    back_cos, back_sin = trig_table(ctx_size, 2 * ctx_size, 2 * ctx_size)
    spec_real = returned_spec[0].reshape(2 * ctx_size, slice_rows * chan_width)
    spec_imag = returned_spec[1].reshape(2 * ctx_size, slice_rows * chan_width)
    block_out = jnp.dot(back_cos, spec_real, precision=HIGH) - jnp.dot(
        back_sin, spec_imag, precision=HIGH
    )
    block_out = block_out.reshape(ctx_size, slice_rows, chan_width)
    returned = lax.all_to_all(block_out, "ctx", split_axis=0, concat_axis=1, tiled=True)
    convolved = returned.reshape(seq_rows, chan_width) / full_length
    mixer = (post_gate.astype(jnp.float32) * (convolved + skip_gain[None, :] * gated_input)).astype(
        jnp.bfloat16
    )
    partial_value = contract_rows(mixer, lax.all_gather(out_weight, "ctx", axis=0, tiled=True))
    projected = lax.psum_scatter(partial_value, "chan", scatter_dimension=1, tiled=True).astype(
        jnp.bfloat16
    )
    return projected


PARTS = 4


def project_kernel(
    mixer_ref, weight_ref, out_ref, held, total, share, near, sent, landed,
    y_send, y_recv, z_send, z_recv, own_send, own_recv, pass_send, pass_recv,
    core_send, core_recv, end_send, end_recv, *, lines
):
    ctx_size, groups, length, mine = held.shape
    group = lax.axis_index("group")
    ctx = lax.axis_index("ctx")
    core = lax.axis_index("chan")
    z, x = ctx // 2, ctx % 2
    step = length // PARTS
    rows = length // ctx_size
    feats = weight_ref.shape[0]
    per_core = ctx_size // 2

    def device(ctx_id, core_id):
        return (group, ctx_id, core_id)

    across = (1 - group, ctx, core)
    beside = device(z * 2 + 1 - x, core)
    sibling = device(ctx, 1 - core)

    barrier = pltpu.get_barrier_semaphore()
    pl.semaphore_signal(barrier, inc=1, device_id=across, device_id_type=MESH)
    pl.semaphore_signal(barrier, inc=1, device_id=sibling, device_id_type=MESH)
    for offset in range(1, ctx_size):
        for core_id in range(2):
            pl.semaphore_signal(
                barrier, inc=1, device_id=device(lax.rem(ctx + offset, ctx_size), core_id),
                device_id_type=MESH,
            )
    pl.semaphore_wait(barrier, 2 * ctx_size)

    def remote(src, dst, send, recv, target):
        return pltpu.make_async_remote_copy(
            src_ref=src, dst_ref=dst, send_sem=send, recv_sem=recv, device_id=target,
            device_id_type=MESH,
        )

    def span(part):
        return pl.ds(part * step, step)

    def y_copy(part):
        return remote(
            mixer_ref.at[1 - group, span(part)], held.at[ctx, group, span(part)],
            y_send.at[part], y_recv.at[part], across,
        )

    def z_copy(offset, part):
        return remote(
            held.at[ctx, :, span(part)], held.at[ctx, :, span(part)],
            z_send.at[offset - 1, part], z_recv.at[offset - 1, part],
            device(lax.rem(z + offset, lines) * 2 + x, core),
        )

    def own_copy(part):
        return remote(
            held.at[ctx, :, span(part)], held.at[ctx, :, span(part)],
            own_send.at[part], own_recv.at[part], beside,
        )

    def pass_copy(offset, part):
        source = lax.rem(z + lines - offset, lines) * 2 + x
        return remote(
            held.at[source, :, span(part)], held.at[source, :, span(part)],
            pass_send.at[offset - 1, part], pass_recv.at[offset - 1, part], beside,
        )

    def core_copy(part):
        return remote(
            share.at[part], near.at[part], core_send.at[part], core_recv.at[part], sibling
        )

    slot = lax.rem(ctx, per_core)
    owner = ctx // per_core

    def end_copy(part):
        return remote(
            sent.at[part], landed.at[slot], end_send.at[part], end_recv.at[slot],
            device(2 * part + core, owner),
        )

    for part in range(PARTS):
        y_copy(part).start()
    for part in range(PARTS):
        held[ctx, group, part * step : (part + 1) * step, :] = mixer_ref[
            group, part * step : (part + 1) * step, :
        ]
    for part in range(PARTS):
        y_copy(part).wait_recv()
        for offset in (2, 1, 3):
            z_copy(offset, part).start()
        own_copy(part).start()

    def relay(part):
        for offset in (1, 3, 2):
            z_copy(offset, part).wait_recv()
            pass_copy(offset, part).start()

    def multiply(part):
        own_copy(part).wait_recv()
        for offset in (1, 3, 2):
            pass_copy(offset, part).wait_recv()
        for source in range(ctx_size):
            block = jnp.concatenate(
                [held[source, g, part * step : (part + 1) * step, :] for g in range(groups)], axis=1
            )
            columns = jnp.concatenate(
                [
                    weight_ref[:, (g * ctx_size + source) * mine : (g * ctx_size + source + 1) * mine]
                    for g in range(groups)
                ],
                axis=1,
            )
            term = contract_rows(block, columns)
            if source == 0:
                total[part] = term
            else:
                total[part] += term
        share[part] = total[part, pl.ds(pl.multiple_of((1 - core) * rows, rows), rows), :]
        core_copy(part).start()

    def finish(part):
        core_copy(part).wait_recv()
        mine_part = total[part, pl.ds(pl.multiple_of(core * rows, rows), rows), :]
        sent[part] = (mine_part + near[part]).astype(sent.dtype)
        here = jnp.logical_and(ctx == 2 * part + core, core == owner)

        @pl.when(here)
        def _():
            landed[slot] = sent[part]

        @pl.when(jnp.logical_not(here))
        def _():
            end_copy(part).start()

    relay(0)
    relay(1)
    multiply(0)
    relay(2)
    multiply(1)
    finish(0)
    relay(3)
    multiply(2)
    finish(1)
    multiply(3)
    finish(2)
    finish(3)

    for source in range(per_core):
        from_here = jnp.logical_and(core * per_core + source == ctx, core == lax.rem(ctx, 2))

        @pl.when(jnp.logical_not(from_here))
        def _():
            remote(
                sent.at[0], landed.at[source], end_send.at[0], end_recv.at[source],
                device(0, 0),
            ).wait_recv()

        out_ref[:, source * feats : (source + 1) * feats] = landed[source]

    for part in range(PARTS):
        y_copy(part).wait_send()
        own_copy(part).wait_send()
        core_copy(part).wait_send()
        for offset in range(1, lines):
            z_copy(offset, part).wait_send()
            pass_copy(offset, part).wait_send()
        here = jnp.logical_and(ctx == 2 * part + core, core == owner)

        @pl.when(jnp.logical_not(here))
        def _():
            end_copy(part).wait_send()


def project(mixer, weight, ctx_size):
    groups, length, mine = mixer.shape
    feats = weight.shape[0]
    rows = length // ctx_size
    lines = ctx_size // 2
    dma = pltpu.SemaphoreType.DMA
    return pl.pallas_call(
        functools.partial(project_kernel, lines=lines),
        out_shape=jax.ShapeDtypeStruct((rows, feats * ctx_size // 2), jnp.bfloat16),
        in_specs=[pl.BlockSpec(memory_space=pltpu.VMEM)] * 2,
        out_specs=pl.BlockSpec(memory_space=pltpu.VMEM),
        scratch_shapes=[
            pltpu.VMEM((ctx_size, groups, length, mine), jnp.bfloat16),
            pltpu.VMEM((PARTS, length // PARTS, feats), jnp.float32),
            pltpu.VMEM((PARTS, rows, feats), jnp.float32),
            pltpu.VMEM((PARTS, rows, feats), jnp.float32),
            pltpu.VMEM((PARTS, rows, feats), jnp.bfloat16),
            pltpu.VMEM((ctx_size // 2, rows, feats), jnp.bfloat16),
            dma((PARTS,)), dma((PARTS,)),
            dma((lines - 1, PARTS)), dma((lines - 1, PARTS)),
            dma((PARTS,)), dma((PARTS,)),
            dma((lines - 1, PARTS)), dma((lines - 1, PARTS)),
            dma((PARTS,)), dma((PARTS,)),
            dma((PARTS,)), dma((ctx_size // 2,)),
        ],
        compiler_params=pltpu.CompilerParams(
            collective_id=0, has_side_effects=True, vmem_limit_bytes=40 * 1024 * 1024
        ),
        name="project",
    )(mixer, weight)


def dft_tables(residues, quotients, positions):
    full_length = residues * quotients
    kept = residues // 2 + 1
    freq = (np.arange(kept)[:, None] + residues * np.arange(quotients)[None, :]).reshape(-1, 1)
    steps = (freq * np.arange(positions)[None, :]) % full_length
    angles = steps * (2.0 * math.pi / full_length)
    table = np.concatenate([np.cos(angles), -np.sin(angles)], axis=0).astype(np.float32)
    high = table.astype(jnp.bfloat16)
    low = (table - high.astype(np.float32)).astype(jnp.bfloat16)
    return np.concatenate([high, low], axis=1)


def convolve_kernel(
    values_ref, pre_ref, post_ref, skip_ref, flip_ref, filter_ref, table_ref, back_ref, out_ref,
    spec_in, table, back, x_out, g_out, f_out, x_all, g_all, f_all, gated, trans, product,
    load, x_send, x_recv, g_send, g_recv, f_send, f_recv
):
    f32, bf16 = jnp.float32, jnp.bfloat16
    groups, length, mine = out_ref.shape
    quotients = flip_ref.shape[0]
    ctx_size = f_all.shape[0]
    peers = groups * ctx_size
    rows = length // ctx_size
    middle = ctx_size
    half = ctx_size * mine
    group = lax.axis_index("group")
    ctx = lax.axis_index("ctx")
    core = lax.axis_index("chan")
    me = group * ctx_size + ctx

    filter_load = pltpu.make_async_copy(
        filter_ref.at[:, :, :, pl.ds(pl.multiple_of(group * half, half), half)], spec_in, load.at[0]
    )
    filter_load.start()
    table_load = pltpu.make_async_copy(table_ref, table, load.at[1])
    table_load.start()
    back_load = pltpu.make_async_copy(back_ref, back, load.at[2])
    back_load.start()

    def device(offset):
        to = lax.rem(me + offset, peers)
        return (to // ctx_size, lax.rem(to, ctx_size), core)

    barrier = pltpu.get_barrier_semaphore()
    for offset in range(1, peers):
        pl.semaphore_signal(barrier, inc=1, device_id=device(offset), device_id_type=MESH)
    for peer in range(peers):
        cols = slice(peer * mine, (peer + 1) * mine)
        x_out[peer] = (values_ref[:, cols].astype(f32) * pre_ref[:, cols].astype(f32)).astype(bf16)
    pl.semaphore_wait(barrier, peers - 1)

    def peer_copy(src, dst, send, recv, offset):
        return pltpu.make_async_remote_copy(
            src_ref=src.at[lax.rem(me + offset, peers)], dst_ref=dst.at[me],
            send_sem=send.at[offset - 1], recv_sem=recv.at[offset - 1],
            device_id=device(offset), device_id_type=MESH,
        )

    def peer_wait(src, dst, send, recv, offset):
        pltpu.make_async_remote_copy(
            src_ref=src.at[0], dst_ref=dst.at[lax.rem(me + peers - offset, peers)],
            send_sem=send.at[offset - 1], recv_sem=recv.at[offset - 1],
            device_id=device(offset), device_id_type=MESH,
        ).wait_recv()

    def filter_copy(offset):
        to = lax.rem(ctx + offset, ctx_size)
        return pltpu.make_async_remote_copy(
            src_ref=f_out.at[to], dst_ref=f_all.at[ctx],
            send_sem=f_send.at[offset - 1], recv_sem=f_recv.at[offset - 1],
            device_id=(group, to, core), device_id_type=MESH,
        )

    def filter_wait(offset):
        pltpu.make_async_remote_copy(
            src_ref=f_out.at[0], dst_ref=f_all.at[lax.rem(ctx + ctx_size - offset, ctx_size)],
            send_sem=f_send.at[offset - 1], recv_sem=f_recv.at[offset - 1],
            device_id=(group, lax.rem(ctx + offset, ctx_size), core), device_id_type=MESH,
        ).wait_recv()

    for offset in range(1, peers):
        peer_copy(x_out, x_all, x_send, x_recv, offset).start()
    filter_load.wait()
    scale = 1.0 / (2 * length)
    for peer in range(ctx_size):
        f_out[peer] = (spec_in[:, :, :, peer * mine : (peer + 1) * mine] * scale).astype(bf16)
    for offset in range(1, ctx_size):
        filter_copy(offset).start()
    for peer in range(peers):
        g_out[peer] = post_ref[:, peer * mine : (peer + 1) * mine]
    for offset in range(1, peers):
        peer_copy(g_out, g_all, g_send, g_recv, offset).start()
    x_all[me] = x_out[me]
    g_all[me] = g_out[me]
    f_all[ctx] = f_out[ctx]

    for offset in range(1, peers):
        peer_wait(x_out, x_all, x_send, x_recv, offset)
    for block in range(ctx_size):
        gated[block * rows : (block + 1) * rows, :] = jnp.concatenate(
            [x_all[g * ctx_size + block] for g in range(groups)], axis=1
        )
    table_load.wait()
    kept = 2 * (middle + 1)

    def forward(row, carry):
        at = pl.ds(pl.multiple_of(row * quotients, quotients), quotients)
        trans[at, :] = jnp.dot(
            table[at, :length], gated[...], preferred_element_type=f32
        ) + jnp.dot(table[at, length:], gated[...], preferred_element_type=f32)
        return carry

    lax.fori_loop(0, kept, forward, 0)

    for offset in range(1, ctx_size):
        filter_wait(offset)
    for residue in range(middle + 1):
        spec = [f_all[residue // 2, part, residue % 2].astype(f32) for part in range(2)]
        if 0 < residue < middle:
            other = 2 * ctx_size - residue
            for part in range(2):
                mirrored = jnp.dot(
                    flip_ref[...], f_all[other // 2, part, other % 2], preferred_element_type=f32
                )
                spec[part] = spec[part] + (mirrored if part == 0 else -mirrored)
        spec_re, spec_im = (jnp.concatenate([s] * groups, axis=1) for s in spec)
        at_re = slice(residue * quotients, (residue + 1) * quotients)
        at_im = slice((middle + 1 + residue) * quotients, (middle + 2 + residue) * quotients)
        re, im = trans[at_re, :], trans[at_im, :]
        product[at_re, :] = (re * spec_re - im * spec_im).astype(bf16)
        product[at_im, :] = (re * spec_im + im * spec_re).astype(bf16)

    back_load.wait()
    for offset in range(1, peers):
        peer_wait(g_out, g_all, g_send, g_recv, offset)
    depth = kept * quotients

    def backward(block, carry):
        at = pl.ds(pl.multiple_of(block * rows, rows), rows)
        convolved = jnp.dot(
            back[at, :depth], product[...], preferred_element_type=f32
        ) + jnp.dot(back[at, depth:], product[...], preferred_element_type=f32)
        whole = convolved + skip_ref[...] * gated[at, :].astype(f32)
        for g in range(groups):
            gate = g_all[g * ctx_size + block].astype(f32)
            out_ref[g, at, :] = (gate * whole[:, g * mine : (g + 1) * mine]).astype(bf16)
        return carry

    lax.fori_loop(0, ctx_size, backward, 0)
    for offset in range(1, peers):
        peer_copy(x_out, x_all, x_send, x_recv, offset).wait_send()
        peer_copy(g_out, g_all, g_send, g_recv, offset).wait_send()
    for offset in range(1, ctx_size):
        filter_copy(offset).wait_send()


def spread(values, pre_gate, post_gate, filter_spectrum, skip_gain, out_weight):
    f32, bf16 = jnp.float32, jnp.bfloat16
    rows, width = values.shape
    groups = lax.axis_size("group")
    ctx_size = lax.axis_size("ctx")
    residues, quotients = 2 * ctx_size, filter_spectrum.shape[2]
    length = rows * ctx_size
    peers = groups * ctx_size
    mine = width // peers
    group_index = lax.axis_index("group")
    ctx_index = lax.axis_index("ctx")
    skip = lax.dynamic_slice_in_dim(
        skip_gain, (group_index * ctx_size + ctx_index) * mine, mine, axis=0
    )
    skip = jnp.tile(skip, groups).reshape(1, groups * mine)
    flip = jnp.asarray(np.eye(quotients, dtype=np.float32)[::-1].astype(bf16))
    table = dft_tables(residues, quotients, length)
    back = np.concatenate([table[:, :length].T, table[:, length:].T], axis=1)
    depth = table.shape[0]
    vmem, dma = pltpu.VMEM, pltpu.SemaphoreType.DMA
    here, there = pl.BlockSpec(memory_space=pltpu.VMEM), pl.BlockSpec(memory_space=pl.ANY)
    mixer = pl.pallas_call(
        convolve_kernel,
        out_shape=jax.ShapeDtypeStruct((groups, length, mine), bf16),
        in_specs=[here] * 5 + [there] * 3,
        out_specs=here,
        scratch_shapes=[
            vmem((2, 2, quotients, width // groups), f32),
            vmem(table.shape, bf16),
            vmem(back.shape, bf16),
            vmem((peers, rows, mine), bf16),
            vmem((peers, rows, mine), bf16),
            vmem((ctx_size, 2, 2, quotients, mine), bf16),
            vmem((peers, rows, mine), bf16),
            vmem((peers, rows, mine), bf16),
            vmem((ctx_size, 2, 2, quotients, mine), bf16),
            vmem((length, groups * mine), bf16),
            vmem((depth, groups * mine), f32),
            vmem((depth, groups * mine), bf16),
            dma((3,)),
            dma((peers - 1,)), dma((peers - 1,)), dma((peers - 1,)), dma((peers - 1,)),
            dma((ctx_size - 1,)), dma((ctx_size - 1,)),
        ],
        compiler_params=pltpu.CompilerParams(
            collective_id=1, has_side_effects=True, vmem_limit_bytes=48 * 1024 * 1024
        ),
        name="convolve",
    )(values, pre_gate, post_gate, skip, flip, filter_spectrum, jnp.asarray(table), jnp.asarray(back))
    return project(mixer, out_weight, ctx_size)


def solution(mesh):
    small = mesh.shape["ctx"] <= 8
    return jax.shard_map(
        spread if small else local,
        mesh=mesh,
        in_specs=(
            P(("group", "ctx"), "chan"),
            P(("group", "ctx"), "chan"),
            P(("group", "ctx"), "chan"),
            P(None, "ctx", None, "chan"),
            P("chan"),
            P("ctx", "chan"),
        ),
        out_specs=P(("group", "ctx"), "chan"),
        check_vma=False,
    )
```

```python
import functools
import math

import jax
import jax.numpy as jnp
import numpy as np
from jax import lax
from jax.experimental import pallas as pl
from jax.experimental.pallas import tpu as pltpu
from jax.sharding import PartitionSpec as P

HIGH = lax.Precision.HIGHEST
MESH = pl.DeviceIdType.MESH


def trig_table(left_count, right_count, modulus):
    left_ids = jnp.arange(left_count, dtype=jnp.int32)[:, None]
    right_ids = jnp.arange(right_count, dtype=jnp.int32)[None, :]
    angles = (left_ids * right_ids % modulus).astype(jnp.float32) * (2.0 * math.pi / modulus)
    return (jnp.cos(angles), jnp.sin(angles))


def rotate(real_part, imag_part, cosine, sine):
    return (real_part * cosine - imag_part * sine, real_part * sine + imag_part * cosine)


def apply_matrix(matrix, operand):
    return jnp.einsum("kt,...tc->...kc", matrix, operand, precision=HIGH)


def local_transform(real_part, imag_part, direction_sign):
    length_now = real_part.shape[-2]
    cosine, sine = trig_table(length_now, length_now, length_now)
    new_real = apply_matrix(cosine, real_part) - direction_sign * apply_matrix(sine, imag_part)
    new_imag = apply_matrix(cosine, imag_part) + direction_sign * apply_matrix(sine, real_part)
    return (new_real, new_imag)


def twiddle(real_part, imag_part, row_ids, freq_ids, full_length, direction_sign):
    angles = (
        (row_ids * freq_ids % full_length).astype(jnp.float32)
        * (2.0 * math.pi / full_length)
        * direction_sign
    )
    return rotate(real_part, imag_part, jnp.cos(angles), jnp.sin(angles))


def contract_rows(activations, weight_piece):
    return lax.dot_general(
        activations, weight_piece, (((1,), (1,)), ((), ())), preferred_element_type=jnp.float32
    )


def local(values, pre_gate, post_gate, filter_spectrum, skip_gain, out_weight):
    seq_rows, chan_width = values.shape
    ctx_size = lax.axis_size("ctx")
    ctx_index = lax.axis_index("ctx")
    slice_rows = seq_rows // ctx_size
    full_length = 2 * seq_rows * ctx_size
    gated_input = values.astype(jnp.float32) * pre_gate.astype(jnp.float32)
    blocks = lax.all_to_all(
        gated_input.reshape(1, seq_rows, chan_width), "ctx", split_axis=1, concat_axis=0, tiled=True
    )
    flat_blocks = blocks.reshape(ctx_size, slice_rows * chan_width)
    block_cos, block_sin = trig_table(2 * ctx_size, ctx_size, 2 * ctx_size)
    real_part = jnp.dot(block_cos, flat_blocks, precision=HIGH).reshape(
        2 * ctx_size, slice_rows, chan_width
    )
    imag_part = -jnp.dot(block_sin, flat_blocks, precision=HIGH).reshape(
        2 * ctx_size, slice_rows, chan_width
    )
    row_ids = (ctx_index * slice_rows + jnp.arange(slice_rows, dtype=jnp.int32)).reshape(
        1, slice_rows, 1
    )
    freq_ids = jnp.arange(2 * ctx_size, dtype=jnp.int32).reshape(2 * ctx_size, 1, 1)
    real_part, imag_part = twiddle(real_part, imag_part, row_ids, freq_ids, full_length, -1.0)
    columns = lax.all_to_all(
        jnp.stack([real_part, imag_part]), "ctx", split_axis=1, concat_axis=2, tiled=True
    )
    real_part, imag_part = local_transform(columns[0], columns[1], -1.0)
    filter_real = filter_spectrum[0]
    filter_imag = filter_spectrum[1]
    product_real = real_part * filter_real - imag_part * filter_imag
    product_imag = real_part * filter_imag + imag_part * filter_real
    product_real, product_imag = local_transform(product_real, product_imag, 1.0)
    own_freq = (2 * ctx_index + jnp.arange(2, dtype=jnp.int32)).reshape(2, 1, 1)
    all_rows = jnp.arange(seq_rows, dtype=jnp.int32).reshape(1, seq_rows, 1)
    product_real, product_imag = twiddle(
        product_real, product_imag, all_rows, own_freq, full_length, 1.0
    )
    returned_spec = lax.all_to_all(
        jnp.stack([product_real, product_imag]), "ctx", split_axis=2, concat_axis=1, tiled=True
    )
    back_cos, back_sin = trig_table(ctx_size, 2 * ctx_size, 2 * ctx_size)
    spec_real = returned_spec[0].reshape(2 * ctx_size, slice_rows * chan_width)
    spec_imag = returned_spec[1].reshape(2 * ctx_size, slice_rows * chan_width)
    block_out = jnp.dot(back_cos, spec_real, precision=HIGH) - jnp.dot(
        back_sin, spec_imag, precision=HIGH
    )
    block_out = block_out.reshape(ctx_size, slice_rows, chan_width)
    returned = lax.all_to_all(block_out, "ctx", split_axis=0, concat_axis=1, tiled=True)
    convolved = returned.reshape(seq_rows, chan_width) / full_length
    mixer = (post_gate.astype(jnp.float32) * (convolved + skip_gain[None, :] * gated_input)).astype(
        jnp.bfloat16
    )
    partial_value = contract_rows(mixer, lax.all_gather(out_weight, "ctx", axis=0, tiled=True))
    projected = lax.psum_scatter(partial_value, "chan", scatter_dimension=1, tiled=True).astype(
        jnp.bfloat16
    )
    return projected


PARTS = 4


def project_kernel(
    mixer_ref, weight_ref, out_ref, held, total, share, near, sent, landed,
    y_send, y_recv, z_send, z_recv, own_send, own_recv, pass_send, pass_recv,
    core_send, core_recv, end_send, end_recv, *, lines
):
    ctx_size, groups, length, mine = held.shape
    group = lax.axis_index("group")
    ctx = lax.axis_index("ctx")
    core = lax.axis_index("chan")
    z, x = ctx // 2, ctx % 2
    step = length // PARTS
    rows = length // ctx_size
    feats = weight_ref.shape[0]
    per_core = ctx_size // 2

    def device(ctx_id, core_id):
        return (group, ctx_id, core_id)

    across = (1 - group, ctx, core)
    beside = device(z * 2 + 1 - x, core)
    sibling = device(ctx, 1 - core)

    barrier = pltpu.get_barrier_semaphore()
    pl.semaphore_signal(barrier, inc=1, device_id=across, device_id_type=MESH)
    pl.semaphore_signal(barrier, inc=1, device_id=sibling, device_id_type=MESH)
    for offset in range(1, ctx_size):
        for core_id in range(2):
            pl.semaphore_signal(
                barrier, inc=1, device_id=device(lax.rem(ctx + offset, ctx_size), core_id),
                device_id_type=MESH,
            )
    pl.semaphore_wait(barrier, 2 * ctx_size)

    def remote(src, dst, send, recv, target):
        return pltpu.make_async_remote_copy(
            src_ref=src, dst_ref=dst, send_sem=send, recv_sem=recv, device_id=target,
            device_id_type=MESH,
        )

    def span(part):
        return pl.ds(part * step, step)

    def y_copy(part):
        return remote(
            mixer_ref.at[1 - group, span(part)], held.at[ctx, group, span(part)],
            y_send.at[part], y_recv.at[part], across,
        )

    def line_index(way, hop):
        return lax.rem(z + (lines - hop if way == 0 else hop), lines) * 2 + x

    def comes(way, hop):
        return z >= hop if way == 0 else z + hop < lines

    def goes_on(way):
        return z + 1 < lines if way == 0 else z > 0

    def line_copy(way, hop, part, source):
        return remote(
            held.at[source, :, span(part)], held.at[source, :, span(part)],
            z_send.at[way * (lines - 1) + hop - 1, part],
            z_recv.at[way * (lines - 1) + hop - 1, part],
            device(line_index(1 - way, 1), core),
        )

    ways = [(hop, way) for hop in range(1, lines) for way in range(2)]

    def own_copy(part):
        return remote(
            held.at[ctx, :, span(part)], held.at[ctx, :, span(part)],
            own_send.at[part], own_recv.at[part], beside,
        )

    def pass_copy(way, hop, part):
        source = line_index(way, hop)
        return remote(
            held.at[source, :, span(part)], held.at[source, :, span(part)],
            pass_send.at[way * (lines - 1) + hop - 1, part],
            pass_recv.at[way * (lines - 1) + hop - 1, part],
            beside,
        )

    def core_copy(part):
        return remote(
            share.at[part], near.at[part], core_send.at[part], core_recv.at[part], sibling
        )

    slot = lax.rem(ctx, per_core)
    owner = ctx // per_core

    def end_copy(part):
        return remote(
            sent.at[part], landed.at[slot], end_send.at[part], end_recv.at[slot],
            device(2 * part + core, owner),
        )

    for part in range(PARTS):
        y_copy(part).start()
    for part in range(PARTS):
        held[ctx, group, part * step : (part + 1) * step, :] = mixer_ref[
            group, part * step : (part + 1) * step, :
        ]
    for part in range(PARTS):
        y_copy(part).wait_recv()
        for way in range(2):

            @pl.when(goes_on(way))
            def _():
                line_copy(way, 1, part, ctx).start()

        own_copy(part).start()

    def relay(turn):
        for hop, way in ways:
            part = turn - (hop - 1)
            if not 0 <= part < PARTS:
                continue

            @pl.when(comes(way, hop))
            def _():
                source = line_index(way, hop)
                line_copy(way, hop, part, source).wait_recv()
                if hop + 1 < lines:

                    @pl.when(goes_on(way))
                    def _():
                        line_copy(way, hop + 1, part, source).start()

                pass_copy(way, hop, part).start()

    def multiply(part):
        own_copy(part).wait_recv()
        for hop, way in ways:

            @pl.when(comes(way, hop))
            def _():
                pass_copy(way, hop, part).wait_recv()

        for source in range(ctx_size):
            block = jnp.concatenate(
                [held[source, g, part * step : (part + 1) * step, :] for g in range(groups)], axis=1
            )
            columns = jnp.concatenate(
                [
                    weight_ref[:, (g * ctx_size + source) * mine : (g * ctx_size + source + 1) * mine]
                    for g in range(groups)
                ],
                axis=1,
            )
            term = contract_rows(block, columns)
            if source == 0:
                total[part] = term
            else:
                total[part] += term
        share[part] = total[part, pl.ds(pl.multiple_of((1 - core) * rows, rows), rows), :]
        core_copy(part).start()

    def finish(part):
        core_copy(part).wait_recv()
        mine_part = total[part, pl.ds(pl.multiple_of(core * rows, rows), rows), :]
        sent[part] = (mine_part + near[part]).astype(sent.dtype)
        here = jnp.logical_and(ctx == 2 * part + core, core == owner)

        @pl.when(here)
        def _():
            landed[slot] = sent[part]

        @pl.when(jnp.logical_not(here))
        def _():
            end_copy(part).start()

    for turn in range(lines - 1):
        relay(turn)
    multiply_at = 0
    for turn in range(lines - 1, PARTS + lines - 2):
        relay(turn)
        multiply(multiply_at)
        if multiply_at:
            finish(multiply_at - 1)
        multiply_at += 1
    for part in range(multiply_at, PARTS):
        multiply(part)
        finish(part - 1)
    finish(PARTS - 1)

    for source in range(per_core):
        from_here = jnp.logical_and(core * per_core + source == ctx, core == lax.rem(ctx, 2))

        @pl.when(jnp.logical_not(from_here))
        def _():
            remote(
                sent.at[0], landed.at[source], end_send.at[0], end_recv.at[source],
                device(0, 0),
            ).wait_recv()

        out_ref[:, source * feats : (source + 1) * feats] = landed[source]

    for part in range(PARTS):
        y_copy(part).wait_send()
        own_copy(part).wait_send()
        core_copy(part).wait_send()
        for hop, way in ways:

            @pl.when(comes(way, hop))
            def _():
                pass_copy(way, hop, part).wait_send()

            @pl.when(jnp.logical_and(comes(way, hop - 1), goes_on(way)))
            def _():
                line_copy(way, hop, part, line_index(way, hop - 1)).wait_send()

        here = jnp.logical_and(ctx == 2 * part + core, core == owner)

        @pl.when(jnp.logical_not(here))
        def _():
            end_copy(part).wait_send()


def project(mixer, weight, ctx_size):
    groups, length, mine = mixer.shape
    feats = weight.shape[0]
    rows = length // ctx_size
    lines = ctx_size // 2
    dma = pltpu.SemaphoreType.DMA
    return pl.pallas_call(
        functools.partial(project_kernel, lines=lines),
        out_shape=jax.ShapeDtypeStruct((rows, feats * ctx_size // 2), jnp.bfloat16),
        in_specs=[pl.BlockSpec(memory_space=pltpu.VMEM)] * 2,
        out_specs=pl.BlockSpec(memory_space=pltpu.VMEM),
        scratch_shapes=[
            pltpu.VMEM((ctx_size, groups, length, mine), jnp.bfloat16),
            pltpu.VMEM((PARTS, length // PARTS, feats), jnp.float32),
            pltpu.VMEM((PARTS, rows, feats), jnp.float32),
            pltpu.VMEM((PARTS, rows, feats), jnp.float32),
            pltpu.VMEM((PARTS, rows, feats), jnp.bfloat16),
            pltpu.VMEM((ctx_size // 2, rows, feats), jnp.bfloat16),
            dma((PARTS,)), dma((PARTS,)),
            dma((2 * (lines - 1), PARTS)), dma((2 * (lines - 1), PARTS)),
            dma((PARTS,)), dma((PARTS,)),
            dma((2 * (lines - 1), PARTS)), dma((2 * (lines - 1), PARTS)),
            dma((PARTS,)), dma((PARTS,)),
            dma((PARTS,)), dma((ctx_size // 2,)),
        ],
        compiler_params=pltpu.CompilerParams(
            collective_id=0, has_side_effects=True, vmem_limit_bytes=40 * 1024 * 1024
        ),
        name="project",
    )(mixer, weight)


def dft_tables(residues, quotients, positions):
    full_length = residues * quotients
    kept = residues // 2 + 1
    freq = (np.arange(kept)[:, None] + residues * np.arange(quotients)[None, :]).reshape(-1, 1)
    steps = (freq * np.arange(positions)[None, :]) % full_length
    angles = steps * (2.0 * math.pi / full_length)
    table = np.concatenate([np.cos(angles), -np.sin(angles)], axis=0).astype(np.float32)
    high = table.astype(jnp.bfloat16)
    low = (table - high.astype(np.float32)).astype(jnp.bfloat16)
    return np.concatenate([high, low], axis=1)


def convolve_kernel(
    values_ref, pre_ref, post_ref, skip_ref, flip_ref, filter_ref, table_ref, back_ref, out_ref,
    spec_in, table, back, x_out, g_out, f_out, x_all, g_all, f_all, gated, trans, product,
    load, x_send, x_recv, g_send, g_recv, f_send, f_recv
):
    f32, bf16 = jnp.float32, jnp.bfloat16
    groups, length, mine = out_ref.shape
    quotients = flip_ref.shape[0]
    ctx_size = f_all.shape[0]
    peers = groups * ctx_size
    rows = length // ctx_size
    middle = ctx_size
    half = ctx_size * mine
    group = lax.axis_index("group")
    ctx = lax.axis_index("ctx")
    core = lax.axis_index("chan")
    me = group * ctx_size + ctx

    filter_load = pltpu.make_async_copy(
        filter_ref.at[:, :, :, pl.ds(pl.multiple_of(group * half, half), half)], spec_in, load.at[0]
    )
    filter_load.start()
    table_load = pltpu.make_async_copy(table_ref, table, load.at[1])
    table_load.start()
    back_load = pltpu.make_async_copy(back_ref, back, load.at[2])
    back_load.start()

    def device(offset):
        to = lax.rem(me + offset, peers)
        return (to // ctx_size, lax.rem(to, ctx_size), core)

    barrier = pltpu.get_barrier_semaphore()
    for offset in range(1, peers):
        pl.semaphore_signal(barrier, inc=1, device_id=device(offset), device_id_type=MESH)
    for peer in range(peers):
        cols = slice(peer * mine, (peer + 1) * mine)
        x_out[peer] = (values_ref[:, cols].astype(f32) * pre_ref[:, cols].astype(f32)).astype(bf16)
    pl.semaphore_wait(barrier, peers - 1)

    def peer_copy(src, dst, send, recv, offset):
        return pltpu.make_async_remote_copy(
            src_ref=src.at[lax.rem(me + offset, peers)], dst_ref=dst.at[me],
            send_sem=send.at[offset - 1], recv_sem=recv.at[offset - 1],
            device_id=device(offset), device_id_type=MESH,
        )

    def peer_wait(src, dst, send, recv, offset):
        pltpu.make_async_remote_copy(
            src_ref=src.at[0], dst_ref=dst.at[lax.rem(me + peers - offset, peers)],
            send_sem=send.at[offset - 1], recv_sem=recv.at[offset - 1],
            device_id=device(offset), device_id_type=MESH,
        ).wait_recv()

    def filter_copy(offset):
        to = lax.rem(ctx + offset, ctx_size)
        return pltpu.make_async_remote_copy(
            src_ref=f_out.at[to], dst_ref=f_all.at[ctx],
            send_sem=f_send.at[offset - 1], recv_sem=f_recv.at[offset - 1],
            device_id=(group, to, core), device_id_type=MESH,
        )

    def filter_wait(offset):
        pltpu.make_async_remote_copy(
            src_ref=f_out.at[0], dst_ref=f_all.at[lax.rem(ctx + ctx_size - offset, ctx_size)],
            send_sem=f_send.at[offset - 1], recv_sem=f_recv.at[offset - 1],
            device_id=(group, lax.rem(ctx + offset, ctx_size), core), device_id_type=MESH,
        ).wait_recv()

    for offset in range(1, peers):
        peer_copy(x_out, x_all, x_send, x_recv, offset).start()
    filter_load.wait()
    scale = 1.0 / (2 * length)
    for peer in range(ctx_size):
        f_out[peer] = (spec_in[:, :, :, peer * mine : (peer + 1) * mine] * scale).astype(bf16)
    for offset in range(1, ctx_size):
        filter_copy(offset).start()
    for peer in range(peers):
        g_out[peer] = post_ref[:, peer * mine : (peer + 1) * mine]
    for offset in range(1, peers):
        peer_copy(g_out, g_all, g_send, g_recv, offset).start()
    x_all[me] = x_out[me]
    g_all[me] = g_out[me]
    f_all[ctx] = f_out[ctx]

    for offset in range(1, peers):
        peer_wait(x_out, x_all, x_send, x_recv, offset)
    for block in range(ctx_size):
        gated[block * rows : (block + 1) * rows, :] = jnp.concatenate(
            [x_all[g * ctx_size + block] for g in range(groups)], axis=1
        )
    table_load.wait()
    kept = 2 * (middle + 1)

    def forward(row, carry):
        at = pl.ds(pl.multiple_of(row * quotients, quotients), quotients)
        trans[at, :] = jnp.dot(
            table[at, :length], gated[...], preferred_element_type=f32
        ) + jnp.dot(table[at, length:], gated[...], preferred_element_type=f32)
        return carry

    lax.fori_loop(0, kept, forward, 0)

    for offset in range(1, ctx_size):
        filter_wait(offset)
    for residue in range(middle + 1):
        spec = [f_all[residue // 2, part, residue % 2].astype(f32) for part in range(2)]
        if 0 < residue < middle:
            other = 2 * ctx_size - residue
            for part in range(2):
                mirrored = jnp.dot(
                    flip_ref[...], f_all[other // 2, part, other % 2], preferred_element_type=f32
                )
                spec[part] = spec[part] + (mirrored if part == 0 else -mirrored)
        spec_re, spec_im = (jnp.concatenate([s] * groups, axis=1) for s in spec)
        at_re = slice(residue * quotients, (residue + 1) * quotients)
        at_im = slice((middle + 1 + residue) * quotients, (middle + 2 + residue) * quotients)
        re, im = trans[at_re, :], trans[at_im, :]
        product[at_re, :] = (re * spec_re - im * spec_im).astype(bf16)
        product[at_im, :] = (re * spec_im + im * spec_re).astype(bf16)

    back_load.wait()
    for offset in range(1, peers):
        peer_wait(g_out, g_all, g_send, g_recv, offset)
    depth = kept * quotients

    def backward(block, carry):
        at = pl.ds(pl.multiple_of(block * rows, rows), rows)
        convolved = jnp.dot(
            back[at, :depth], product[...], preferred_element_type=f32
        ) + jnp.dot(back[at, depth:], product[...], preferred_element_type=f32)
        whole = convolved + skip_ref[...] * gated[at, :].astype(f32)
        for g in range(groups):
            gate = g_all[g * ctx_size + block].astype(f32)
            out_ref[g, at, :] = (gate * whole[:, g * mine : (g + 1) * mine]).astype(bf16)
        return carry

    lax.fori_loop(0, ctx_size, backward, 0)
    for offset in range(1, peers):
        peer_copy(x_out, x_all, x_send, x_recv, offset).wait_send()
        peer_copy(g_out, g_all, g_send, g_recv, offset).wait_send()
    for offset in range(1, ctx_size):
        filter_copy(offset).wait_send()


def spread(values, pre_gate, post_gate, filter_spectrum, skip_gain, out_weight):
    f32, bf16 = jnp.float32, jnp.bfloat16
    rows, width = values.shape
    groups = lax.axis_size("group")
    ctx_size = lax.axis_size("ctx")
    residues, quotients = 2 * ctx_size, filter_spectrum.shape[2]
    length = rows * ctx_size
    peers = groups * ctx_size
    mine = width // peers
    group_index = lax.axis_index("group")
    ctx_index = lax.axis_index("ctx")
    skip = lax.dynamic_slice_in_dim(
        skip_gain, (group_index * ctx_size + ctx_index) * mine, mine, axis=0
    )
    skip = jnp.tile(skip, groups).reshape(1, groups * mine)
    flip = jnp.asarray(np.eye(quotients, dtype=np.float32)[::-1].astype(bf16))
    table = dft_tables(residues, quotients, length)
    back = np.concatenate([table[:, :length].T, table[:, length:].T], axis=1)
    depth = table.shape[0]
    vmem, dma = pltpu.VMEM, pltpu.SemaphoreType.DMA
    here, there = pl.BlockSpec(memory_space=pltpu.VMEM), pl.BlockSpec(memory_space=pl.ANY)
    mixer = pl.pallas_call(
        convolve_kernel,
        out_shape=jax.ShapeDtypeStruct((groups, length, mine), bf16),
        in_specs=[here] * 5 + [there] * 3,
        out_specs=here,
        scratch_shapes=[
            vmem((2, 2, quotients, width // groups), f32),
            vmem(table.shape, bf16),
            vmem(back.shape, bf16),
            vmem((peers, rows, mine), bf16),
            vmem((peers, rows, mine), bf16),
            vmem((ctx_size, 2, 2, quotients, mine), bf16),
            vmem((peers, rows, mine), bf16),
            vmem((peers, rows, mine), bf16),
            vmem((ctx_size, 2, 2, quotients, mine), bf16),
            vmem((length, groups * mine), bf16),
            vmem((depth, groups * mine), f32),
            vmem((depth, groups * mine), bf16),
            dma((3,)),
            dma((peers - 1,)), dma((peers - 1,)), dma((peers - 1,)), dma((peers - 1,)),
            dma((ctx_size - 1,)), dma((ctx_size - 1,)),
        ],
        compiler_params=pltpu.CompilerParams(
            collective_id=1, has_side_effects=True, vmem_limit_bytes=48 * 1024 * 1024
        ),
        name="convolve",
    )(values, pre_gate, post_gate, skip, flip, filter_spectrum, jnp.asarray(table), jnp.asarray(back))
    return project(mixer, out_weight, ctx_size)


def solution(mesh):
    small = mesh.shape["ctx"] <= 8
    return jax.shard_map(
        spread if small else local,
        mesh=mesh,
        in_specs=(
            P(("group", "ctx"), "chan"),
            P(("group", "ctx"), "chan"),
            P(("group", "ctx"), "chan"),
            P(None, "ctx", None, "chan"),
            P("chan"),
            P("ctx", "chan"),
        ),
        out_specs=P(("group", "ctx"), "chan"),
        check_vma=False,
    )
```
